32 devices in a mesh: ctx: 8 (over z, x), head: 4 (over y, core).
Axes of the slice: x: 2, y: 2, z: 4, core: 2. Of those that a mesh axis runs over, the one named last changes fastest.
Arguments:
- query: bfloat16 [1024, 2048], P('ctx', 'head'), may hold values from -5 to 5, as said below
- key: bfloat16 [1024, 128], P('ctx'), may hold values from -5 to 5, as said below
- value: bfloat16 [1024, 128], P('ctx'), may hold values from -6 to 6
- grad_out: bfloat16 [1024, 2048], P('ctx', 'head'), may hold values from -6 to 6
- doc_lengths: int32 [32], replicated, may hold values from 1 to 64, 1024 in all
Outputs:
- attention_out: bfloat16 [1024, 2048], P('ctx', 'head')
- grad_query: bfloat16 [1024, 2048], P('ctx', 'head')
- grad_key: bfloat16 [1024, 128], P('ctx')
- grad_value: bfloat16 [1024, 128], P('ctx')
The draws below stay inside these ranges and needn't reach their ends.
Inputs may be any that keep to these rules, and one draw needn't show every extreme that they name: `doc_lengths`: positive lengths of the documents in sequence order, summing to 1024; the longest is exactly 64. `query`: real values. `key`: real values.
All inputs are finite; a program needn't handle non-finite values.
Results may differ from the reference program's by a relative error of at most 0.014.
Values may be sent and summed in bfloat16 or wider, within the bound.
A program may use at most 64 MiB of HBM per device.

```python
import math
import jax
import jax.numpy as jnp
import numpy as np
from jax import lax

HD = 128
HEADS = 16
STRETCH = 64
DOCS = 32
REACH = 1
TOK_DEV = 128
TOKENS = 1024
MOST = 64
N_CTX = 8


def draw_query(key, part):
    base = jax.random.fold_in(key, 11)
    result = jnp.clip(jax.random.normal(base, (TOKENS, HEADS * HD), jnp.float32), -5.0, 5.0)
    return result.astype(jnp.bfloat16)


def draw_key(key, part):
    base = jax.random.fold_in(key, 23)
    result = jnp.clip(jax.random.normal(base, (TOKENS, HD), jnp.float32), -5.0, 5.0)
    return result.astype(jnp.bfloat16)


def level_of(stream_key, dims, split, least, high):
    factor_of = 1.0
    for position, shards_of in split:
        heights = jax.random.uniform(jax.random.fold_in(jax.random.fold_in(stream_key, 6), position), (shards_of,), jnp.float32, least / len(split), high / len(split))
        factor_of = factor_of * jnp.repeat(jnp.exp(heights), dims[position] // shards_of).reshape((-1,) + (1,) * (len(dims) - 1 - position))
    return factor_of


def length_profile(amount, total, most, lean):
    loads = [(1 << 20) // math.isqrt(rank ** lean) + 1 for rank in range(2, amount + 1)]
    surplus, given = total - most - (amount - 1), [1] * (amount - 1)
    while surplus > 0:
        movable = [i for i in range(amount - 1) if given[i] < most]
        whole, left = sum([loads[i] for i in movable]), surplus
        for i in movable:
            more = min(most - given[i], max(1, left * loads[i] // whole), surplus)
            given[i] = given[i] + more
            surplus = surplus - more
    return np.array([most] + given)


def uneven_parts(rng, number_of, total, most, slope):
    if number_of == 2:
        one = jax.random.randint(rng, (), max(1, total - most), min(most, total - 1) + 1)
        return jnp.stack([one, total - one])
    tallies = jnp.asarray(length_profile(number_of, total, most, slope), jnp.int32)
    couples = (number_of - 1) // 2
    giver, taker = tallies[1:1 + 2 * couples:2], tallies[2:2 + 2 * couples:2]
    room = jnp.minimum(giver - 1, most - taker)
    shifted = jax.random.randint(jax.random.fold_in(rng, 1), (couples,), 0, 1 << 20) % (room + 1)
    tallies = tallies.at[1:1 + 2 * couples:2].set(giver - shifted).at[2:2 + 2 * couples:2].set(taker + shifted)
    return tallies[jax.random.permutation(jax.random.fold_in(rng, 2), number_of)]


def centred(key, extent, scale, reach, split=(), kind=jnp.bfloat16):
    drawn = scale * jax.random.normal(key, extent, jnp.float32)
    if split:
        drawn = drawn * level_of(key, extent, split, -0.22, 0.18)
    return jnp.clip(drawn, -reach, reach).astype(kind)


def setup_inputs(seed: int = 0) -> dict:
    arg_keys = jax.random.split(jax.random.key(seed), 6)
    query = draw_query(jax.random.fold_in(arg_keys[5], 71), 0)
    key = draw_key(jax.random.fold_in(arg_keys[5], 71), 0)
    value = centred(arg_keys[2], (TOKENS, HD), 1.0, 6.0, ((0, 8),))
    grad_out = centred(arg_keys[3], (TOKENS, HEADS * HD), 1.0, 6.0, ((0, 8), (1, 4)))
    doc_lengths = uneven_parts(arg_keys[4], DOCS, TOKENS, MOST, 2).astype(jnp.int32)
    return {"query": query, "key": key, "value": value, "grad_out": grad_out, "doc_lengths": doc_lengths}


def reference(query, key, value, grad_out, doc_lengths):
    seq_index = jnp.arange(TOKENS, dtype=jnp.int32)
    stretch_id = seq_index // STRETCH
    lower_half = stretch_id < N_CTX
    device_id = jnp.where(lower_half, stretch_id, 2 * N_CTX - 1 - stretch_id)
    shard_row = device_id * TOK_DEV + jnp.where(lower_half, 0, STRETCH) + seq_index % STRETCH
    local_row = seq_index % TOK_DEV
    owner_dev = seq_index // TOK_DEV
    back_stretch = jnp.where(local_row < STRETCH, owner_dev, 2 * N_CTX - 1 - owner_dev)
    back_pos = (back_stretch * STRETCH + local_row % STRETCH).astype(jnp.int32)
    queries = jnp.take(query, shard_row, axis=0).reshape(TOKENS, HEADS, HD)
    cotangent = jnp.take(grad_out, shard_row, axis=0).reshape(TOKENS, HEADS, HD)
    keys = jnp.take(key, shard_row, axis=0)
    values_seq = jnp.take(value, shard_row, axis=0)
    doc_ends = jnp.cumsum(doc_lengths).astype(jnp.int32)
    doc_ids = jnp.sum((doc_ends[None, :] <= seq_index[:, None]).astype(jnp.int32), axis=1)
    margin = REACH * STRETCH
    window = margin + STRETCH
    key_pad = jnp.concatenate([jnp.zeros((margin, HD), key.dtype), keys], axis=0)
    value_pad = jnp.concatenate([jnp.zeros((margin, HD), value.dtype), values_seq], axis=0)
    doc_pad = jnp.concatenate([jnp.full((margin,), -1, jnp.int32), doc_ids], axis=0)
    score_scale = HD ** -0.5

    def stretch_step(carry, stretch_index):
        grad_k_acc, grad_v_acc = carry
        start = (stretch_index * STRETCH).astype(jnp.int32)
        q_block = lax.dynamic_slice_in_dim(queries, start, STRETCH, 0).astype(jnp.float32)
        dout_block = lax.dynamic_slice_in_dim(cotangent, start, STRETCH, 0).astype(jnp.float32)
        q_docs = lax.dynamic_slice_in_dim(doc_ids, start, STRETCH, 0)
        q_pos = start + jnp.arange(STRETCH, dtype=jnp.int32)
        k_block = lax.dynamic_slice_in_dim(key_pad, start, window, 0).astype(jnp.float32)
        v_block = lax.dynamic_slice_in_dim(value_pad, start, window, 0).astype(jnp.float32)
        k_docs = lax.dynamic_slice_in_dim(doc_pad, start, window, 0)
        k_pos = start - margin + jnp.arange(window, dtype=jnp.int32)
        live_mask = (k_docs[None, :] == q_docs[:, None]) & (k_pos[None, :] <= q_pos[:, None]) & (k_pos[None, :] >= 0)
        live_mask = live_mask[None]
        scores = jnp.einsum("qhd,kd->hqk", q_block, k_block) * score_scale
        row_max = jnp.max(jnp.where(live_mask, scores, -1e30), axis=2)
        row_sum = jnp.sum(jnp.where(live_mask, jnp.exp(scores - row_max[:, :, None]), 0.0), axis=2)
        log_sum = row_max + jnp.log(row_sum)
        weights = jnp.where(live_mask, jnp.exp(scores - log_sum[:, :, None]), 0.0)
        probs = lax.optimization_barrier(weights.astype(jnp.bfloat16)).astype(jnp.float32)
        out_block = jnp.einsum("hqk,kd->qhd", probs, v_block).astype(jnp.bfloat16)
        delta = jnp.sum(dout_block * out_block.astype(jnp.float32), axis=2).T
        dprobs = jnp.einsum("qhd,kd->hqk", dout_block, v_block)
        dscores = (weights * (dprobs - delta[:, :, None]) * score_scale).astype(jnp.bfloat16)
        dscores = lax.optimization_barrier(dscores).astype(jnp.float32)
        q_grad = jnp.einsum("hqk,kd->qhd", dscores, k_block).astype(jnp.bfloat16)
        k_grad = jnp.einsum("hqk,qhd->kd", dscores, q_block)
        v_grad = jnp.einsum("hqk,qhd->kd", probs, dout_block)
        grad_k_acc = lax.dynamic_update_slice_in_dim(grad_k_acc, lax.dynamic_slice_in_dim(grad_k_acc, start, window, 0) + k_grad, start, 0)
        grad_v_acc = lax.dynamic_update_slice_in_dim(grad_v_acc, lax.dynamic_slice_in_dim(grad_v_acc, start, window, 0) + v_grad, start, 0)
        return (grad_k_acc, grad_v_acc), (out_block, q_grad)

    start_acc = jnp.zeros((TOKENS + margin, HD), jnp.float32)
    (grad_k_acc, grad_v_acc), (out_blocks, q_grads) = lax.scan(stretch_step, (start_acc, start_acc), jnp.arange(TOKENS // STRETCH, dtype=jnp.int32))
    attention_seq = out_blocks.reshape(TOKENS, HEADS * HD)
    grad_q_seq = q_grads.reshape(TOKENS, HEADS * HD)
    grad_k_seq = grad_k_acc[margin:].astype(jnp.bfloat16)
    grad_v_seq = grad_v_acc[margin:].astype(jnp.bfloat16)
    return (jnp.take(attention_seq, back_pos, axis=0), jnp.take(grad_q_seq, back_pos, axis=0),
            jnp.take(grad_k_seq, back_pos, axis=0), jnp.take(grad_v_seq, back_pos, axis=0))
```

```python
import functools

import jax
import jax.numpy as jnp
from jax import lax
from jax.experimental import pallas as pl
from jax.experimental.pallas import tpu as pltpu
from jax.sharding import PartitionSpec as P


def from_behind(array, axis, by):
    size = lax.axis_size(axis)
    pairs = [(i, i + by) for i in range(size) if 0 <= i + by < size]
    return lax.ppermute(array, axis, pairs)


def fold_home(key_parts, upward):
    slot_count = key_parts.shape[0]
    slots = [jnp.zeros(key_parts.shape[1:], jnp.float32)]
    slots += [key_parts[i] for i in range(slot_count)]
    for bit_index in range(slot_count.bit_length()):
        offset = 1 << bit_index
        moving = [slot for slot in range(slot_count + 1) if slot & offset]
        sent = jnp.stack([slots[slot] for slot in moving]).astype(jnp.bfloat16)
        arrived = from_behind(sent, "ctx", offset if upward else -offset).astype(jnp.float32)
        for i, slot in enumerate(moving):
            slots[slot] = jnp.zeros_like(slots[slot])
            slots[slot - offset] = slots[slot - offset] + arrived[i]
    return slots[0]


def body(query, key, value, grad_out, doc_lengths):
    tok_dev = key.shape[0]
    stretch_len = tok_dev // 2
    head_width = key.shape[1]
    head_count = query.shape[1] // head_width
    score_scale = head_width ** (-0.5)
    n_context = lax.axis_size("ctx")
    reach_count = n_context // 8
    my_index = lax.axis_index("ctx")
    docs = jnp.arange(doc_lengths.shape[0])
    doc_ends = jnp.sum(jnp.where(docs[None, :] <= docs[:, None], doc_lengths[None, :], 0), axis=1)

    def positions(first_row, row_count):
        global_row = first_row + jnp.arange(row_count, dtype=jnp.int32)
        owner_index = global_row // tok_dev
        inner_row = global_row % tok_dev
        stretch_id = jnp.where(
            inner_row < stretch_len, owner_index, 2 * n_context - 1 - owner_index
        )
        seq_place = stretch_id * stretch_len + inner_row % stretch_len
        inside = (owner_index >= 0) & (owner_index < n_context)
        seq_place = jnp.where(inside, seq_place, -1)
        doc_ids = jnp.sum((doc_ends[None, :] <= seq_place[:, None]).astype(jnp.int32), axis=1)
        return (seq_place, doc_ids)

    q_place, q_docs = positions(my_index * tok_dev, tok_dev)
    packed = jnp.concatenate([key, value], axis=1)
    queries = query.reshape(tok_dev, head_count, head_width)
    cotangent = grad_out.reshape(tok_dev, head_count, head_width)
    q_spans = [(0, tok_dev)]

    def live_pairs(k_place, k_docs, q_start, q_count):
        return (
            (k_docs[None, :] == q_docs[q_start : q_start + q_count, None])
            & (k_place[None, :] <= q_place[q_start : q_start + q_count, None])
            & (k_place[None, :] >= 0)
        )

    def tile_scores(key_block):
        return (
            jnp.einsum("rhd,kd->hrk", queries, key_block, preferred_element_type=jnp.float32)
            * score_scale
        )

    def add_stats(running, kv_block, k_place, k_docs):
        row_max, row_sum = running
        key_block = kv_block[:, :head_width]
        q_start, q_count = q_spans[0]
        live_mask = live_pairs(k_place, k_docs, q_start, q_count)

        def tile_stats(q_start=q_start, q_count=q_count, live_mask=live_mask):
            scores = tile_scores(key_block)
            tile_peak = jnp.max(jnp.where(live_mask[None], scores, -1e30), axis=2)
            tile_mass = jnp.sum(
                jnp.where(live_mask[None], jnp.exp(scores - tile_peak[:, :, None]), 0.0), axis=2
            )
            return (tile_peak, tile_mass)

        tile_peak, tile_mass = tile_stats()
        old_max = row_max
        new_max = jnp.maximum(old_max, tile_peak)
        merged = row_sum * jnp.exp(old_max - new_max) + tile_mass * jnp.exp(tile_peak - new_max)
        row_sum = row_sum.at[:, q_start : q_start + q_count].set(merged)
        row_max = row_max.at[:, q_start : q_start + q_count].set(new_max)
        return (row_max, row_sum)

    def sweep(update, initial):
        running = update(initial, packed, q_place, q_docs)

        def cycle_step(carried, step_index):
            running, kv_lower, kv_upper = carried
            kv_lower = from_behind(kv_lower, "ctx", 1)
            kv_upper = from_behind(kv_upper, "ctx", -1)
            k_place, k_docs = positions((my_index - step_index) * tok_dev, tok_dev)
            running = update(running, kv_lower, k_place, k_docs)
            k_place, k_docs = positions((my_index + step_index) * tok_dev, tok_dev)
            running = update(running, kv_upper, k_place, k_docs)
            return ((running, kv_lower, kv_upper), None)

        (running, kv_lower, kv_upper), unused = lax.scan(
            cycle_step, (running, packed, packed), jnp.arange(1, reach_count + 1, dtype=jnp.int32)
        )
        return running

    initial_stats = (
        jnp.full((head_count, tok_dev), -1e30, jnp.float32),
        jnp.zeros((head_count, tok_dev), jnp.float32),
    )
    row_max, row_sum = sweep(add_stats, initial_stats)
    log_sum = row_max + jnp.log(row_sum)

    def add_output(out_acc, kv_block, k_place, k_docs):
        key_block = kv_block[:, :head_width]
        value_block = kv_block[:, head_width:]
        q_start, q_count = q_spans[0]
        live_mask = live_pairs(k_place, k_docs, q_start, q_count)

        def tile_output(q_start=q_start, q_count=q_count, live_mask=live_mask):
            scores = tile_scores(key_block)
            weights = jnp.where(
                live_mask[None],
                jnp.exp(scores - log_sum[:, q_start : q_start + q_count, None]),
                0.0,
            )
            probs = weights.astype(jnp.bfloat16)
            return jnp.einsum("hrk,kd->rhd", probs, value_block, preferred_element_type=jnp.float32)

        out_acc = out_acc.at[q_start : q_start + q_count].add(tile_output())
        return out_acc

    out_acc = sweep(add_output, jnp.zeros((tok_dev, head_count, head_width), jnp.float32))
    attention = out_acc.astype(jnp.bfloat16)
    delta = jnp.sum(cotangent.astype(jnp.float32) * attention.astype(jnp.float32), axis=2).T

    def grads_of(grad_q_acc, kv_block, k_place, k_docs):
        key_block = kv_block[:, :head_width]
        value_block = kv_block[:, head_width:]
        q_start, q_count = q_spans[0]
        live_mask = live_pairs(k_place, k_docs, q_start, q_count)

        def tile_grads(q_start=q_start, q_count=q_count, live_mask=live_mask):
            scores = tile_scores(key_block)
            weights = jnp.where(
                live_mask[None],
                jnp.exp(scores - log_sum[:, q_start : q_start + q_count, None]),
                0.0,
            )
            probs = weights.astype(jnp.bfloat16)
            dprobs = jnp.einsum(
                "rhd,kd->hrk", cotangent, value_block, preferred_element_type=jnp.float32
            )
            dscores = (
                weights * (dprobs - delta[:, q_start : q_start + q_count, None]) * score_scale
            ).astype(jnp.bfloat16)
            q_part = jnp.einsum(
                "hrk,kd->rhd", dscores, key_block, preferred_element_type=jnp.float32
            )
            k_part = jnp.einsum("hrk,rhd->kd", dscores, queries, preferred_element_type=jnp.float32)
            v_part = jnp.einsum("hrk,rhd->kd", probs, cotangent, preferred_element_type=jnp.float32)
            return (q_part, jnp.concatenate([k_part, v_part], axis=1))

        q_part, tile_part = tile_grads()
        grad_q_acc = grad_q_acc.at[q_start : q_start + q_count].add(q_part)
        return (grad_q_acc, tile_part)

    grad_q_acc, own_part = grads_of(
        jnp.zeros((tok_dev, head_count, head_width), jnp.float32), packed, q_place, q_docs
    )

    def back_step(carried, step_index):
        grad_q_acc, kv_lower, kv_upper = carried
        kv_lower = from_behind(kv_lower, "ctx", 1)
        kv_upper = from_behind(kv_upper, "ctx", -1)
        k_place, k_docs = positions((my_index - step_index) * tok_dev, tok_dev)
        grad_q_acc, lower_part = grads_of(grad_q_acc, kv_lower, k_place, k_docs)
        k_place, k_docs = positions((my_index + step_index) * tok_dev, tok_dev)
        grad_q_acc, upper_part = grads_of(grad_q_acc, kv_upper, k_place, k_docs)
        return ((grad_q_acc, kv_lower, kv_upper), (lower_part, upper_part))

    (grad_q_acc, kv_lower, kv_upper), (lower_parts, upper_parts) = lax.scan(
        back_step, (grad_q_acc, packed, packed), jnp.arange(1, reach_count + 1, dtype=jnp.int32)
    )
    from_lower = fold_home(lower_parts, False)
    from_upper = fold_home(upper_parts, True)
    kv_total = own_part + from_lower + from_upper
    kv_total = lax.psum(kv_total.astype(jnp.bfloat16), "head").astype(jnp.float32)
    kv_grads = kv_total.astype(jnp.bfloat16)
    attention_out = attention.reshape(tok_dev, head_count * head_width)
    grad_query = grad_q_acc.astype(jnp.bfloat16).reshape(tok_dev, head_count * head_width)
    return (attention_out, grad_query, kv_grads[:, :head_width], kv_grads[:, head_width:])


MESH = pl.DeviceIdType.MESH
NT = (((1,), (1,)), ((), ()))
TN = (((0,), (0,)), ((), ()))
NN = (((1,), (0,)), ((), ()))


def dot(lhs, rhs, dims):
    return lax.dot_general(lhs, rhs, dims, preferred_element_type=jnp.float32)


def near_kernel(
    n_ctx,
    n_head,
    lens_ref,
    q_hbm,
    k_hbm,
    v_hbm,
    g_hbm,
    o_ref,
    dq_ref,
    dk_ref,
    dv_ref,
    q_ref,
    g_ref,
    kv_ref,
    halo_ref,
    own_part,
    own_send,
    halo_send,
    own_recv,
    halo_recv,
    final,
    load_sem,
    kv_send_sem,
    kv_recv_sem,
    own_send_sem,
    own_recv_sem,
    hs_send_sem,
    hs_recv_sem,
    fin_send_sem,
    fin_recv_sem,
):
    c = lax.axis_index("ctx")
    h = lax.axis_index("head")
    width = k_hbm.shape[1]
    tok = k_hbm.shape[0]
    st = tok // 2
    heads = q_hbm.shape[1] // width
    rows = heads * st
    quarter = tok // n_head
    per_half = n_head // 2
    has_prev = c > 0
    has_next = c < n_ctx - 1

    barrier = pltpu.get_barrier_semaphore()
    for d in range(1, n_head):
        pl.semaphore_signal(
            barrier, inc=1, device_id=(c, lax.rem(h + d, n_head)), device_id_type=MESH
        )

    @pl.when(has_prev)
    def _():
        for d in range(n_head):
            pl.semaphore_signal(barrier, inc=1, device_id=(c - 1, d), device_id_type=MESH)

    @pl.when(has_next)
    def _():
        for d in range(n_head):
            pl.semaphore_signal(barrier, inc=1, device_id=(c + 1, d), device_id_type=MESH)

    loads = [
        pltpu.make_async_copy(k_hbm, kv_ref.at[:, pl.ds(0, width)], load_sem.at[0]),
        pltpu.make_async_copy(v_hbm, kv_ref.at[:, pl.ds(width, width)], load_sem.at[1]),
        pltpu.make_async_copy(q_hbm, q_ref, load_sem.at[2]),
        pltpu.make_async_copy(g_hbm, g_ref, load_sem.at[3]),
    ]
    for load in loads:
        load.start()

    lane = lax.broadcasted_iota(jnp.int32, (1, rows), 1)
    place = lax.rem(lane, st)
    key_row = lax.broadcasted_iota(jnp.int32, (2 * st, rows), 0)
    bases = (c * st, (2 * n_ctx - 1 - c) * st)
    starts = [jnp.zeros((1, rows), jnp.int32) for _ in bases]
    doc_end = jnp.int32(0)
    for doc in range(lens_ref.shape[0]):
        doc_end = doc_end + lens_ref[doc]
        for i, base in enumerate(bases):
            starts[i] = jnp.where(place + base >= doc_end, doc_end, starts[i])
    live = [
        (key_row + (base - st) >= start) & (key_row - st <= place)
        for base, start in zip(bases, starts)
    ]

    loads[0].wait()
    loads[1].wait()
    pl.semaphore_wait(
        barrier,
        (n_head - 1) + n_head * has_prev.astype(jnp.int32) + n_head * has_next.astype(jnp.int32),
    )

    def kv_copy(part, step):
        return pltpu.make_async_remote_copy(
            src_ref=kv_ref.at[pl.ds(part * st, st), :],
            dst_ref=halo_ref.at[part],
            send_sem=kv_send_sem.at[part],
            recv_sem=kv_recv_sem.at[part],
            device_id=(c + step, h),
            device_id_type=MESH,
        )

    lower_kv, upper_kv = kv_copy(0, 1), kv_copy(1, -1)

    @pl.when(has_next)
    def _():
        lower_kv.start()

    @pl.when(has_prev)
    def _():
        upper_kv.start()

    loads[2].wait()
    loads[3].wait()

    def stacked(ref, part):
        return jnp.concatenate(
            [
                ref[part * st : (part + 1) * st, i * width : (i + 1) * width]
                for i in range(heads)
            ],
            axis=0,
        )

    qs = [stacked(q_ref, part) for part in range(2)]
    gs = [stacked(g_ref, part) for part in range(2)]
    k_own = [kv_ref[part * st : (part + 1) * st, :width] for part in range(2)]
    v_own = [kv_ref[part * st : (part + 1) * st, width:] for part in range(2)]
    s_own = [dot(k_own[part], qs[part], NT) for part in range(2)]
    dp_own = [dot(v_own[part], gs[part], NT) for part in range(2)]

    @pl.when(has_prev)
    def _():
        lower_kv.wait_recv()

    @pl.when(has_next)
    def _():
        upper_kv.wait_recv()

    zero = jnp.zeros((st, 2 * width), jnp.bfloat16)
    halos = [
        jnp.where(has_prev, halo_ref[0], zero),
        jnp.where(has_next, halo_ref[1], kv_ref[0:st, :]),
    ]
    scale = width ** (-0.5)
    probs, dscores, keys, values, grads = [], [], [], [], []
    for part in range(2):
        k_halo, v_halo = halos[part][:, :width], halos[part][:, width:]
        scores = jnp.concatenate([dot(k_halo, qs[part], NT), s_own[part]], axis=0) * scale
        dprobs = jnp.concatenate([dot(v_halo, gs[part], NT), dp_own[part]], axis=0)
        scores = jnp.where(live[part], scores, -1e30)
        peak = jnp.max(scores, axis=0, keepdims=True)
        raw = jnp.where(live[part], jnp.exp(scores - peak), 0.0)
        weights = raw * (1.0 / jnp.sum(raw, axis=0, keepdims=True))
        prob = weights.astype(jnp.bfloat16)
        delta = jnp.sum(prob.astype(jnp.float32) * dprobs, axis=0, keepdims=True)
        dscore = (weights * (dprobs - delta) * scale).astype(jnp.bfloat16)
        grad_k = dot(dscore, qs[part], NN)
        grad_v = dot(prob, gs[part], NN)
        probs.append(prob)
        dscores.append(dscore)
        keys.append(jnp.concatenate([k_halo, k_own[part]], axis=0))
        values.append(jnp.concatenate([v_halo, v_own[part]], axis=0))
        grads.append(jnp.concatenate([grad_k, grad_v], axis=1))

    lower = grads[0][st:] + jnp.where(has_next, 0.0, grads[1][:st])
    own_part[0:st, :] = lower
    own_part[st:tok, :] = grads[1][st:]
    own_send[0:st, :] = lower.astype(jnp.bfloat16)
    own_send[st:tok, :] = grads[1][st:].astype(jnp.bfloat16)
    halo_send[0] = grads[0][:st].astype(jnp.bfloat16)
    halo_send[1] = grads[1][:st].astype(jnp.bfloat16)

    def halo_copy(part, j, step):
        return pltpu.make_async_remote_copy(
            src_ref=halo_send.at[part, pl.ds(j * quarter, quarter), :],
            dst_ref=halo_recv.at[h],
            send_sem=hs_send_sem.at[part, j],
            recv_sem=hs_recv_sem.at[h],
            device_id=(c + step, part * per_half + j),
            device_id_type=MESH,
        )

    down = [halo_copy(0, j, -1) for j in range(per_half)]
    up = [halo_copy(1, j, 1) for j in range(per_half)]

    @pl.when(has_prev)
    def _():
        for copy in down:
            copy.start()

    @pl.when(has_next)
    def _():
        for copy in up:
            copy.start()

    own_copies = []
    for d in range(1, n_head):
        peer = lax.rem(h + d, n_head)
        own_copies.append(
            pltpu.make_async_remote_copy(
                src_ref=own_send.at[pl.ds(pl.multiple_of(peer * quarter, quarter), quarter), :],
                dst_ref=own_recv.at[d - 1],
                send_sem=own_send_sem.at[d - 1],
                recv_sem=own_recv_sem.at[d - 1],
                device_id=(c, peer),
                device_id_type=MESH,
            )
        )
    for copy in own_copies:
        copy.start()

    for part in range(2):
        out = dot(probs[part], values[part], TN).astype(jnp.bfloat16)
        grad_q = dot(dscores[part], keys[part], TN).astype(jnp.bfloat16)
        for i in range(heads):
            where = (slice(part * st, (part + 1) * st), slice(i * width, (i + 1) * width))
            o_ref[where] = out[i * st : (i + 1) * st]
            dq_ref[where] = grad_q[i * st : (i + 1) * st]

    mine = pl.ds(pl.multiple_of(h * quarter, quarter), quarter)
    gets_halo = jnp.where(h < per_half, has_next.astype(jnp.int32), has_prev.astype(jnp.int32))

    @pl.when(gets_halo == 1)
    def _():
        for j in range(n_head):
            pltpu.make_async_remote_copy(
                src_ref=halo_recv.at[j],
                dst_ref=halo_recv.at[j],
                send_sem=hs_send_sem.at[0, 0],
                recv_sem=hs_recv_sem.at[j],
                device_id=(c, lax.rem(h + 1, n_head)),
                device_id_type=MESH,
            ).wait_recv()

    total = own_part[mine, :]
    for d in range(n_head - 1):
        own_copies[d].wait_recv()
        total = total + own_recv[d].astype(jnp.float32)
    near = halo_recv[0].astype(jnp.float32)
    for j in range(1, n_head):
        near = near + halo_recv[j].astype(jnp.float32)
    total = total + jnp.where(gets_halo == 1, near, 0.0)
    final[mine, :] = total.astype(jnp.bfloat16)

    fin_copies = []
    for d in range(1, n_head):
        fin_copies.append(
            pltpu.make_async_remote_copy(
                src_ref=final.at[mine, :],
                dst_ref=final.at[mine, :],
                send_sem=fin_send_sem.at[d - 1],
                recv_sem=fin_recv_sem.at[d - 1],
                device_id=(c, lax.rem(h + d, n_head)),
                device_id_type=MESH,
            )
        )
    for copy in fin_copies:
        copy.start()

    @pl.when(has_next)
    def _():
        lower_kv.wait_send()
        for copy in up:
            copy.wait_send()

    @pl.when(has_prev)
    def _():
        upper_kv.wait_send()
        for copy in down:
            copy.wait_send()

    for copy in own_copies:
        copy.wait_send()
    for d in range(1, n_head):
        sender = lax.rem(h + n_head - d, n_head)
        theirs = pl.ds(pl.multiple_of(sender * quarter, quarter), quarter)
        pltpu.make_async_remote_copy(
            src_ref=final.at[theirs, :],
            dst_ref=final.at[theirs, :],
            send_sem=fin_send_sem.at[d - 1],
            recv_sem=fin_recv_sem.at[d - 1],
            device_id=(c, lax.rem(h + d, n_head)),
            device_id_type=MESH,
        ).wait_recv()
    dk_ref[...] = final[:, :width]
    dv_ref[...] = final[:, width:]
    for copy in fin_copies:
        copy.wait_send()


def near_body(n_ctx, n_head, query, key, value, grad_out, doc_lengths):
    tok, width = key.shape
    st = tok // 2
    quarter = tok // n_head
    bf16, f32 = jnp.bfloat16, jnp.float32
    dma = pltpu.SemaphoreType.DMA
    vmem = pl.BlockSpec(memory_space=pltpu.VMEM)
    hbm = pl.BlockSpec(memory_space=pl.ANY)
    return pl.pallas_call(
        functools.partial(near_kernel, n_ctx, n_head),
        out_shape=(
            jax.ShapeDtypeStruct(query.shape, bf16),
            jax.ShapeDtypeStruct(query.shape, bf16),
            jax.ShapeDtypeStruct(key.shape, bf16),
            jax.ShapeDtypeStruct(key.shape, bf16),
        ),
        in_specs=[pl.BlockSpec(memory_space=pltpu.SMEM), hbm, hbm, hbm, hbm],
        out_specs=(vmem, vmem, vmem, vmem),
        scratch_shapes=[
            pltpu.VMEM(query.shape, bf16),
            pltpu.VMEM(query.shape, bf16),
            pltpu.VMEM((tok, 2 * width), bf16),
            pltpu.VMEM((2, st, 2 * width), bf16),
            pltpu.VMEM((tok, 2 * width), f32),
            pltpu.VMEM((tok, 2 * width), bf16),
            pltpu.VMEM((2, st, 2 * width), bf16),
            pltpu.VMEM((n_head - 1, quarter, 2 * width), bf16),
            pltpu.VMEM((n_head, quarter, 2 * width), bf16),
            pltpu.VMEM((tok, 2 * width), bf16),
            dma((4,)),
            dma((2,)),
            dma((2,)),
            dma((n_head - 1,)),
            dma((n_head - 1,)),
            dma((2, n_head // 2)),
            dma((n_head,)),
            dma((n_head - 1,)),
            dma((n_head - 1,)),
        ],
        compiler_params=pltpu.CompilerParams(
            collective_id=0, has_side_effects=True, vmem_limit_bytes=16 * 1024 * 1024
        ),
    )(doc_lengths, query, key, value, grad_out)


def solution(mesh):
    in_specs = (P("ctx", "head"), P("ctx", None), P("ctx", None), P("ctx", "head"), P())
    out_specs = (P("ctx", "head"), P("ctx", "head"), P("ctx", None), P("ctx", None))
    n_ctx, n_head = mesh.shape["ctx"], mesh.shape["head"]
    run = functools.partial(near_body, n_ctx, n_head) if n_ctx // 8 == 1 else body
    return jax.shard_map(run, mesh=mesh, in_specs=in_specs, out_specs=out_specs, check_vma=False)
```

```python
import functools

import jax
import jax.numpy as jnp
from jax import lax
from jax.experimental import pallas as pl
from jax.experimental.pallas import tpu as pltpu
from jax.sharding import PartitionSpec as P


def from_behind(array, axis, by):
    size = lax.axis_size(axis)
    pairs = [(i, i + by) for i in range(size) if 0 <= i + by < size]
    return lax.ppermute(array, axis, pairs)


def fold_home(key_parts, upward):
    slot_count = key_parts.shape[0]
    slots = [jnp.zeros(key_parts.shape[1:], jnp.float32)]
    slots += [key_parts[i] for i in range(slot_count)]
    for bit_index in range(slot_count.bit_length()):
        offset = 1 << bit_index
        moving = [slot for slot in range(slot_count + 1) if slot & offset]
        sent = jnp.stack([slots[slot] for slot in moving]).astype(jnp.bfloat16)
        arrived = from_behind(sent, "ctx", offset if upward else -offset).astype(jnp.float32)
        for i, slot in enumerate(moving):
            slots[slot] = jnp.zeros_like(slots[slot])
            slots[slot - offset] = slots[slot - offset] + arrived[i]
    return slots[0]


def body(query, key, value, grad_out, doc_lengths):
    tok_dev = key.shape[0]
    stretch_len = tok_dev // 2
    head_width = key.shape[1]
    head_count = query.shape[1] // head_width
    score_scale = head_width ** (-0.5)
    n_context = lax.axis_size("ctx")
    reach_count = n_context // 8
    my_index = lax.axis_index("ctx")
    docs = jnp.arange(doc_lengths.shape[0])
    doc_ends = jnp.sum(jnp.where(docs[None, :] <= docs[:, None], doc_lengths[None, :], 0), axis=1)

    def positions(first_row, row_count):
        global_row = first_row + jnp.arange(row_count, dtype=jnp.int32)
        owner_index = global_row // tok_dev
        inner_row = global_row % tok_dev
        stretch_id = jnp.where(
            inner_row < stretch_len, owner_index, 2 * n_context - 1 - owner_index
        )
        seq_place = stretch_id * stretch_len + inner_row % stretch_len
        inside = (owner_index >= 0) & (owner_index < n_context)
        seq_place = jnp.where(inside, seq_place, -1)
        doc_ids = jnp.sum((doc_ends[None, :] <= seq_place[:, None]).astype(jnp.int32), axis=1)
        return (seq_place, doc_ids)

    q_place, q_docs = positions(my_index * tok_dev, tok_dev)
    packed = jnp.concatenate([key, value], axis=1)
    queries = query.reshape(tok_dev, head_count, head_width)
    cotangent = grad_out.reshape(tok_dev, head_count, head_width)
    q_spans = [(0, tok_dev)]

    def live_pairs(k_place, k_docs, q_start, q_count):
        return (
            (k_docs[None, :] == q_docs[q_start : q_start + q_count, None])
            & (k_place[None, :] <= q_place[q_start : q_start + q_count, None])
            & (k_place[None, :] >= 0)
        )

    def tile_scores(key_block):
        return (
            jnp.einsum("rhd,kd->hrk", queries, key_block, preferred_element_type=jnp.float32)
            * score_scale
        )

    def add_stats(running, kv_block, k_place, k_docs):
        row_max, row_sum = running
        key_block = kv_block[:, :head_width]
        q_start, q_count = q_spans[0]
        live_mask = live_pairs(k_place, k_docs, q_start, q_count)

        def tile_stats(q_start=q_start, q_count=q_count, live_mask=live_mask):
            scores = tile_scores(key_block)
            tile_peak = jnp.max(jnp.where(live_mask[None], scores, -1e30), axis=2)
            tile_mass = jnp.sum(
                jnp.where(live_mask[None], jnp.exp(scores - tile_peak[:, :, None]), 0.0), axis=2
            )
            return (tile_peak, tile_mass)

        tile_peak, tile_mass = tile_stats()
        old_max = row_max
        new_max = jnp.maximum(old_max, tile_peak)
        merged = row_sum * jnp.exp(old_max - new_max) + tile_mass * jnp.exp(tile_peak - new_max)
        row_sum = row_sum.at[:, q_start : q_start + q_count].set(merged)
        row_max = row_max.at[:, q_start : q_start + q_count].set(new_max)
        return (row_max, row_sum)

    def sweep(update, initial):
        running = update(initial, packed, q_place, q_docs)

        def cycle_step(carried, step_index):
            running, kv_lower, kv_upper = carried
            kv_lower = from_behind(kv_lower, "ctx", 1)
            kv_upper = from_behind(kv_upper, "ctx", -1)
            k_place, k_docs = positions((my_index - step_index) * tok_dev, tok_dev)
            running = update(running, kv_lower, k_place, k_docs)
            k_place, k_docs = positions((my_index + step_index) * tok_dev, tok_dev)
            running = update(running, kv_upper, k_place, k_docs)
            return ((running, kv_lower, kv_upper), None)

        (running, kv_lower, kv_upper), unused = lax.scan(
            cycle_step, (running, packed, packed), jnp.arange(1, reach_count + 1, dtype=jnp.int32)
        )
        return running

    initial_stats = (
        jnp.full((head_count, tok_dev), -1e30, jnp.float32),
        jnp.zeros((head_count, tok_dev), jnp.float32),
    )
    row_max, row_sum = sweep(add_stats, initial_stats)
    log_sum = row_max + jnp.log(row_sum)

    def add_output(out_acc, kv_block, k_place, k_docs):
        key_block = kv_block[:, :head_width]
        value_block = kv_block[:, head_width:]
        q_start, q_count = q_spans[0]
        live_mask = live_pairs(k_place, k_docs, q_start, q_count)

        def tile_output(q_start=q_start, q_count=q_count, live_mask=live_mask):
            scores = tile_scores(key_block)
            weights = jnp.where(
                live_mask[None],
                jnp.exp(scores - log_sum[:, q_start : q_start + q_count, None]),
                0.0,
            )
            probs = weights.astype(jnp.bfloat16)
            return jnp.einsum("hrk,kd->rhd", probs, value_block, preferred_element_type=jnp.float32)

        out_acc = out_acc.at[q_start : q_start + q_count].add(tile_output())
        return out_acc

    out_acc = sweep(add_output, jnp.zeros((tok_dev, head_count, head_width), jnp.float32))
    attention = out_acc.astype(jnp.bfloat16)
    delta = jnp.sum(cotangent.astype(jnp.float32) * attention.astype(jnp.float32), axis=2).T

    def grads_of(grad_q_acc, kv_block, k_place, k_docs):
        key_block = kv_block[:, :head_width]
        value_block = kv_block[:, head_width:]
        q_start, q_count = q_spans[0]
        live_mask = live_pairs(k_place, k_docs, q_start, q_count)

        def tile_grads(q_start=q_start, q_count=q_count, live_mask=live_mask):
            scores = tile_scores(key_block)
            weights = jnp.where(
                live_mask[None],
                jnp.exp(scores - log_sum[:, q_start : q_start + q_count, None]),
                0.0,
            )
            probs = weights.astype(jnp.bfloat16)
            dprobs = jnp.einsum(
                "rhd,kd->hrk", cotangent, value_block, preferred_element_type=jnp.float32
            )
            dscores = (
                weights * (dprobs - delta[:, q_start : q_start + q_count, None]) * score_scale
            ).astype(jnp.bfloat16)
            q_part = jnp.einsum(
                "hrk,kd->rhd", dscores, key_block, preferred_element_type=jnp.float32
            )
            k_part = jnp.einsum("hrk,rhd->kd", dscores, queries, preferred_element_type=jnp.float32)
            v_part = jnp.einsum("hrk,rhd->kd", probs, cotangent, preferred_element_type=jnp.float32)
            return (q_part, jnp.concatenate([k_part, v_part], axis=1))

        q_part, tile_part = tile_grads()
        grad_q_acc = grad_q_acc.at[q_start : q_start + q_count].add(q_part)
        return (grad_q_acc, tile_part)

    grad_q_acc, own_part = grads_of(
        jnp.zeros((tok_dev, head_count, head_width), jnp.float32), packed, q_place, q_docs
    )

    def back_step(carried, step_index):
        grad_q_acc, kv_lower, kv_upper = carried
        kv_lower = from_behind(kv_lower, "ctx", 1)
        kv_upper = from_behind(kv_upper, "ctx", -1)
        k_place, k_docs = positions((my_index - step_index) * tok_dev, tok_dev)
        grad_q_acc, lower_part = grads_of(grad_q_acc, kv_lower, k_place, k_docs)
        k_place, k_docs = positions((my_index + step_index) * tok_dev, tok_dev)
        grad_q_acc, upper_part = grads_of(grad_q_acc, kv_upper, k_place, k_docs)
        return ((grad_q_acc, kv_lower, kv_upper), (lower_part, upper_part))

    (grad_q_acc, kv_lower, kv_upper), (lower_parts, upper_parts) = lax.scan(
        back_step, (grad_q_acc, packed, packed), jnp.arange(1, reach_count + 1, dtype=jnp.int32)
    )
    from_lower = fold_home(lower_parts, False)
    from_upper = fold_home(upper_parts, True)
    kv_total = own_part + from_lower + from_upper
    kv_total = lax.psum(kv_total.astype(jnp.bfloat16), "head").astype(jnp.float32)
    kv_grads = kv_total.astype(jnp.bfloat16)
    attention_out = attention.reshape(tok_dev, head_count * head_width)
    grad_query = grad_q_acc.astype(jnp.bfloat16).reshape(tok_dev, head_count * head_width)
    return (attention_out, grad_query, kv_grads[:, :head_width], kv_grads[:, head_width:])


MESH = pl.DeviceIdType.MESH
NT = (((1,), (1,)), ((), ()))
TN = (((0,), (0,)), ((), ()))
NN = (((1,), (0,)), ((), ()))


def dot(lhs, rhs, dims):
    return lax.dot_general(lhs, rhs, dims, preferred_element_type=jnp.float32)


def near_kernel(
    n_ctx,
    n_head,
    lens_hbm,
    q_hbm,
    k_hbm,
    v_hbm,
    g_hbm,
    o_ref,
    dq_ref,
    dk_ref,
    dv_ref,
    lens_ref,
    q_ref,
    g_ref,
    kv_ref,
    halo_ref,
    own_part,
    own_send,
    halo_send,
    own_recv,
    halo_recv,
    final,
    load_sem,
    kv_send_sem,
    kv_recv_sem,
    own_send_sem,
    own_recv_sem,
    hs_send_sem,
    hs_recv_sem,
    fin_send_sem,
    fin_recv_sem,
):
    c = lax.axis_index("ctx")
    h = lax.axis_index("head")
    width = k_hbm.shape[1]
    tok = k_hbm.shape[0]
    st = tok // 2
    heads = q_hbm.shape[1] // width
    rows = heads * st
    quarter = tok // n_head
    per_half = n_head // 2
    has_prev = c > 0
    has_next = c < n_ctx - 1

    barrier = pltpu.get_barrier_semaphore()
    for d in range(1, n_head):
        pl.semaphore_signal(
            barrier, inc=1, device_id=(c, lax.rem(h + d, n_head)), device_id_type=MESH
        )

    @pl.when(has_prev)
    def _():
        for d in range(n_head):
            pl.semaphore_signal(barrier, inc=1, device_id=(c - 1, d), device_id_type=MESH)

    @pl.when(has_next)
    def _():
        for d in range(n_head):
            pl.semaphore_signal(barrier, inc=1, device_id=(c + 1, d), device_id_type=MESH)

    loads = [
        pltpu.make_async_copy(k_hbm, kv_ref.at[:, pl.ds(0, width)], load_sem.at[0]),
        pltpu.make_async_copy(v_hbm, kv_ref.at[:, pl.ds(width, width)], load_sem.at[1]),
        pltpu.make_async_copy(lens_hbm, lens_ref, load_sem.at[2]),
        pltpu.make_async_copy(q_hbm, q_ref, load_sem.at[3]),
        pltpu.make_async_copy(g_hbm, g_ref, load_sem.at[4]),
    ]
    for load in loads:
        load.start()

    loads[0].wait()
    loads[1].wait()
    pl.semaphore_wait(
        barrier,
        (n_head - 1) + n_head * has_prev.astype(jnp.int32) + n_head * has_next.astype(jnp.int32),
    )

    def kv_copy(part, step):
        return pltpu.make_async_remote_copy(
            src_ref=kv_ref.at[pl.ds(part * st, st), :],
            dst_ref=halo_ref.at[part],
            send_sem=kv_send_sem.at[part],
            recv_sem=kv_recv_sem.at[part],
            device_id=(c + step, h),
            device_id_type=MESH,
        )

    lower_kv, upper_kv = kv_copy(0, 1), kv_copy(1, -1)

    @pl.when(has_next)
    def _():
        lower_kv.start()

    @pl.when(has_prev)
    def _():
        upper_kv.start()

    loads[2].wait()
    lane = lax.broadcasted_iota(jnp.int32, (1, rows), 1)
    place = lax.rem(lane, st)
    key_row = lax.broadcasted_iota(jnp.int32, (2 * st, rows), 0)
    bases = (c * st, (2 * n_ctx - 1 - c) * st)
    starts = [jnp.zeros((1, rows), jnp.int32) for _ in bases]
    doc_end = jnp.int32(0)
    for doc in range(lens_ref.shape[0]):
        doc_end = doc_end + lens_ref[doc]
        for i, base in enumerate(bases):
            starts[i] = jnp.where(place + base >= doc_end, doc_end, starts[i])
    live = [
        (key_row + (base - st) >= start) & (key_row - st <= place)
        for base, start in zip(bases, starts)
    ]

    loads[3].wait()
    loads[4].wait()

    def stacked(ref, part):
        return jnp.concatenate(
            [
                ref[part * st : (part + 1) * st, i * width : (i + 1) * width]
                for i in range(heads)
            ],
            axis=0,
        )

    qs = [stacked(q_ref, part) for part in range(2)]
    gs = [stacked(g_ref, part) for part in range(2)]
    k_own = [kv_ref[part * st : (part + 1) * st, :width] for part in range(2)]
    v_own = [kv_ref[part * st : (part + 1) * st, width:] for part in range(2)]
    s_own = [dot(k_own[part], qs[part], NT) for part in range(2)]
    dp_own = [dot(v_own[part], gs[part], NT) for part in range(2)]

    @pl.when(has_prev)
    def _():
        lower_kv.wait_recv()

    @pl.when(has_next)
    def _():
        upper_kv.wait_recv()

    zero = jnp.zeros((st, 2 * width), jnp.bfloat16)
    halos = [
        jnp.where(has_prev, halo_ref[0], zero),
        jnp.where(has_next, halo_ref[1], kv_ref[0:st, :]),
    ]
    scale = width ** (-0.5)
    probs, dscores, keys, values, grads = [], [], [], [], []
    for part in range(2):
        k_halo, v_halo = halos[part][:, :width], halos[part][:, width:]
        scores = jnp.concatenate([dot(k_halo, qs[part], NT), s_own[part]], axis=0) * scale
        dprobs = jnp.concatenate([dot(v_halo, gs[part], NT), dp_own[part]], axis=0)
        scores = jnp.where(live[part], scores, -1e30)
        peak = jnp.max(scores, axis=0, keepdims=True)
        raw = jnp.where(live[part], jnp.exp(scores - peak), 0.0)
        weights = raw * (1.0 / jnp.sum(raw, axis=0, keepdims=True))
        prob = weights.astype(jnp.bfloat16)
        delta = jnp.sum(prob.astype(jnp.float32) * dprobs, axis=0, keepdims=True)
        dscore = (weights * (dprobs - delta) * scale).astype(jnp.bfloat16)
        grad_k = dot(dscore, qs[part], NN)
        grad_v = dot(prob, gs[part], NN)
        probs.append(prob)
        dscores.append(dscore)
        keys.append(jnp.concatenate([k_halo, k_own[part]], axis=0))
        values.append(jnp.concatenate([v_halo, v_own[part]], axis=0))
        grads.append(jnp.concatenate([grad_k, grad_v], axis=1))

    lower = grads[0][st:] + jnp.where(has_next, 0.0, grads[1][:st])
    own_part[0:st, :] = lower
    own_part[st:tok, :] = grads[1][st:]
    own_send[0:st, :] = lower.astype(jnp.bfloat16)
    own_send[st:tok, :] = grads[1][st:].astype(jnp.bfloat16)
    halo_send[0] = grads[0][:st].astype(jnp.bfloat16)
    halo_send[1] = grads[1][:st].astype(jnp.bfloat16)

    def halo_copy(part, j, step):
        return pltpu.make_async_remote_copy(
            src_ref=halo_send.at[part, pl.ds(j * quarter, quarter), :],
            dst_ref=halo_recv.at[h],
            send_sem=hs_send_sem.at[part, j],
            recv_sem=hs_recv_sem.at[h],
            device_id=(c + step, part * per_half + j),
            device_id_type=MESH,
        )

    down = [halo_copy(0, j, -1) for j in range(per_half)]
    up = [halo_copy(1, j, 1) for j in range(per_half)]

    @pl.when(has_prev)
    def _():
        for copy in down:
            copy.start()

    @pl.when(has_next)
    def _():
        for copy in up:
            copy.start()

    own_copies = []
    for d in range(1, n_head):
        peer = lax.rem(h + d, n_head)
        own_copies.append(
            pltpu.make_async_remote_copy(
                src_ref=own_send.at[pl.ds(pl.multiple_of(peer * quarter, quarter), quarter), :],
                dst_ref=own_recv.at[d - 1],
                send_sem=own_send_sem.at[d - 1],
                recv_sem=own_recv_sem.at[d - 1],
                device_id=(c, peer),
                device_id_type=MESH,
            )
        )
    for copy in own_copies:
        copy.start()

    for part in range(2):
        out = dot(probs[part], values[part], TN).astype(jnp.bfloat16)
        grad_q = dot(dscores[part], keys[part], TN).astype(jnp.bfloat16)
        for i in range(heads):
            where = (slice(part * st, (part + 1) * st), slice(i * width, (i + 1) * width))
            o_ref[where] = out[i * st : (i + 1) * st]
            dq_ref[where] = grad_q[i * st : (i + 1) * st]

    mine = pl.ds(pl.multiple_of(h * quarter, quarter), quarter)
    gets_halo = jnp.where(h < per_half, has_next.astype(jnp.int32), has_prev.astype(jnp.int32))

    @pl.when(gets_halo == 1)
    def _():
        for j in range(n_head):
            pltpu.make_async_remote_copy(
                src_ref=halo_recv.at[j],
                dst_ref=halo_recv.at[j],
                send_sem=hs_send_sem.at[0, 0],
                recv_sem=hs_recv_sem.at[j],
                device_id=(c, lax.rem(h + 1, n_head)),
                device_id_type=MESH,
            ).wait_recv()

    total = own_part[mine, :]
    for d in range(n_head - 1):
        own_copies[d].wait_recv()
        total = total + own_recv[d].astype(jnp.float32)
    near = halo_recv[0].astype(jnp.float32)
    for j in range(1, n_head):
        near = near + halo_recv[j].astype(jnp.float32)
    total = total + jnp.where(gets_halo == 1, near, 0.0)
    final[mine, :] = total.astype(jnp.bfloat16)

    fin_copies = []
    for d in range(1, n_head):
        fin_copies.append(
            pltpu.make_async_remote_copy(
                src_ref=final.at[mine, :],
                dst_ref=final.at[mine, :],
                send_sem=fin_send_sem.at[d - 1],
                recv_sem=fin_recv_sem.at[d - 1],
                device_id=(c, lax.rem(h + d, n_head)),
                device_id_type=MESH,
            )
        )
    for copy in fin_copies:
        copy.start()

    @pl.when(has_next)
    def _():
        lower_kv.wait_send()
        for copy in up:
            copy.wait_send()

    @pl.when(has_prev)
    def _():
        upper_kv.wait_send()
        for copy in down:
            copy.wait_send()

    for copy in own_copies:
        copy.wait_send()
    for d in range(1, n_head):
        sender = lax.rem(h + n_head - d, n_head)
        theirs = pl.ds(pl.multiple_of(sender * quarter, quarter), quarter)
        pltpu.make_async_remote_copy(
            src_ref=final.at[theirs, :],
            dst_ref=final.at[theirs, :],
            send_sem=fin_send_sem.at[d - 1],
            recv_sem=fin_recv_sem.at[d - 1],
            device_id=(c, lax.rem(h + d, n_head)),
            device_id_type=MESH,
        ).wait_recv()
    dk_ref[...] = final[:, :width]
    dv_ref[...] = final[:, width:]
    for copy in fin_copies:
        copy.wait_send()


def write_kernel(*refs):
    sources, targets, sems = refs[:4], refs[4:8], refs[8]
    copies = [
        pltpu.make_async_copy(source, target, sems.at[i])
        for i, (source, target) in enumerate(zip(sources, targets))
    ]
    for copy in copies:
        copy.start()
    for copy in copies:
        copy.wait()


def near_body(n_ctx, n_head, query, key, value, grad_out, doc_lengths):
    tok, width = key.shape
    st = tok // 2
    quarter = tok // n_head
    bf16, f32 = jnp.bfloat16, jnp.float32
    dma = pltpu.SemaphoreType.DMA
    vmem = pl.BlockSpec(memory_space=pltpu.VMEM)
    hbm = pl.BlockSpec(memory_space=pltpu.HBM)
    results = pl.pallas_call(
        functools.partial(near_kernel, n_ctx, n_head),
        out_shape=(
            pltpu.VMEM(query.shape, bf16),
            pltpu.VMEM(query.shape, bf16),
            pltpu.VMEM(key.shape, bf16),
            pltpu.VMEM(key.shape, bf16),
        ),
        in_specs=[hbm] * 5,
        out_specs=(vmem,) * 4,
        scratch_shapes=[
            pltpu.SMEM(doc_lengths.shape, jnp.int32),
            pltpu.VMEM(query.shape, bf16),
            pltpu.VMEM(query.shape, bf16),
            pltpu.VMEM((tok, 2 * width), bf16),
            pltpu.VMEM((2, st, 2 * width), bf16),
            pltpu.VMEM((tok, 2 * width), f32),
            pltpu.VMEM((tok, 2 * width), bf16),
            pltpu.VMEM((2, st, 2 * width), bf16),
            pltpu.VMEM((n_head - 1, quarter, 2 * width), bf16),
            pltpu.VMEM((n_head, quarter, 2 * width), bf16),
            pltpu.VMEM((tok, 2 * width), bf16),
            dma((5,)),
            dma((2,)),
            dma((2,)),
            dma((n_head - 1,)),
            dma((n_head - 1,)),
            dma((2, n_head // 2)),
            dma((n_head,)),
            dma((n_head - 1,)),
            dma((n_head - 1,)),
        ],
        compiler_params=pltpu.CompilerParams(
            collective_id=0, has_side_effects=True, vmem_limit_bytes=60 * 1024 * 1024
        ),
    )(doc_lengths, query, key, value, grad_out)
    return pl.pallas_call(
        write_kernel,
        out_shape=tuple(jax.ShapeDtypeStruct(a.shape, bf16) for a in (query, query, key, key)),
        in_specs=[vmem] * 4,
        out_specs=(hbm,) * 4,
        scratch_shapes=[dma((4,))],
        compiler_params=pltpu.CompilerParams(vmem_limit_bytes=1024 * 1024),
        name="write_out",
    )(*results)


def solution(mesh):
    in_specs = (P("ctx", "head"), P("ctx", None), P("ctx", None), P("ctx", "head"), P())
    out_specs = (P("ctx", "head"), P("ctx", "head"), P("ctx", None), P("ctx", None))
    n_ctx, n_head = mesh.shape["ctx"], mesh.shape["head"]
    run = functools.partial(near_body, n_ctx, n_head) if n_ctx // 8 == 1 else body
    return jax.shard_map(run, mesh=mesh, in_specs=in_specs, out_specs=out_specs, check_vma=False)
```

```python
import functools

import jax
import jax.numpy as jnp
from jax import lax
from jax.experimental import pallas as pl
from jax.experimental.pallas import tpu as pltpu
from jax.sharding import PartitionSpec as P


def from_behind(array, axis, by):
    size = lax.axis_size(axis)
    pairs = [(i, i + by) for i in range(size) if 0 <= i + by < size]
    return lax.ppermute(array, axis, pairs)


def fold_home(key_parts, upward):
    slot_count = key_parts.shape[0]
    slots = [jnp.zeros(key_parts.shape[1:], jnp.float32)]
    slots += [key_parts[i] for i in range(slot_count)]
    for bit_index in range(slot_count.bit_length()):
        offset = 1 << bit_index
        moving = [slot for slot in range(slot_count + 1) if slot & offset]
        sent = jnp.stack([slots[slot] for slot in moving]).astype(jnp.bfloat16)
        arrived = from_behind(sent, "ctx", offset if upward else -offset).astype(jnp.float32)
        for i, slot in enumerate(moving):
            slots[slot] = jnp.zeros_like(slots[slot])
            slots[slot - offset] = slots[slot - offset] + arrived[i]
    return slots[0]


def body(query, key, value, grad_out, doc_lengths):
    tok_dev = key.shape[0]
    stretch_len = tok_dev // 2
    head_width = key.shape[1]
    head_count = query.shape[1] // head_width
    score_scale = head_width ** (-0.5)
    n_context = lax.axis_size("ctx")
    reach_count = n_context // 8
    my_index = lax.axis_index("ctx")
    docs = jnp.arange(doc_lengths.shape[0])
    doc_ends = jnp.sum(jnp.where(docs[None, :] <= docs[:, None], doc_lengths[None, :], 0), axis=1)

    def positions(first_row, row_count):
        global_row = first_row + jnp.arange(row_count, dtype=jnp.int32)
        owner_index = global_row // tok_dev
        inner_row = global_row % tok_dev
        stretch_id = jnp.where(
            inner_row < stretch_len, owner_index, 2 * n_context - 1 - owner_index
        )
        seq_place = stretch_id * stretch_len + inner_row % stretch_len
        inside = (owner_index >= 0) & (owner_index < n_context)
        seq_place = jnp.where(inside, seq_place, -1)
        doc_ids = jnp.sum((doc_ends[None, :] <= seq_place[:, None]).astype(jnp.int32), axis=1)
        return (seq_place, doc_ids)

    q_place, q_docs = positions(my_index * tok_dev, tok_dev)
    packed = jnp.concatenate([key, value], axis=1)
    queries = query.reshape(tok_dev, head_count, head_width)
    cotangent = grad_out.reshape(tok_dev, head_count, head_width)
    q_spans = [(0, tok_dev)]

    def live_pairs(k_place, k_docs, q_start, q_count):
        return (
            (k_docs[None, :] == q_docs[q_start : q_start + q_count, None])
            & (k_place[None, :] <= q_place[q_start : q_start + q_count, None])
            & (k_place[None, :] >= 0)
        )

    def tile_scores(key_block):
        return (
            jnp.einsum("rhd,kd->hrk", queries, key_block, preferred_element_type=jnp.float32)
            * score_scale
        )

    def add_stats(running, kv_block, k_place, k_docs):
        row_max, row_sum = running
        key_block = kv_block[:, :head_width]
        q_start, q_count = q_spans[0]
        live_mask = live_pairs(k_place, k_docs, q_start, q_count)

        def tile_stats(q_start=q_start, q_count=q_count, live_mask=live_mask):
            scores = tile_scores(key_block)
            tile_peak = jnp.max(jnp.where(live_mask[None], scores, -1e30), axis=2)
            tile_mass = jnp.sum(
                jnp.where(live_mask[None], jnp.exp(scores - tile_peak[:, :, None]), 0.0), axis=2
            )
            return (tile_peak, tile_mass)

        tile_peak, tile_mass = tile_stats()
        old_max = row_max
        new_max = jnp.maximum(old_max, tile_peak)
        merged = row_sum * jnp.exp(old_max - new_max) + tile_mass * jnp.exp(tile_peak - new_max)
        row_sum = row_sum.at[:, q_start : q_start + q_count].set(merged)
        row_max = row_max.at[:, q_start : q_start + q_count].set(new_max)
        return (row_max, row_sum)

    def sweep(update, initial):
        running = update(initial, packed, q_place, q_docs)

        def cycle_step(carried, step_index):
            running, kv_lower, kv_upper = carried
            kv_lower = from_behind(kv_lower, "ctx", 1)
            kv_upper = from_behind(kv_upper, "ctx", -1)
            k_place, k_docs = positions((my_index - step_index) * tok_dev, tok_dev)
            running = update(running, kv_lower, k_place, k_docs)
            k_place, k_docs = positions((my_index + step_index) * tok_dev, tok_dev)
            running = update(running, kv_upper, k_place, k_docs)
            return ((running, kv_lower, kv_upper), None)

        (running, kv_lower, kv_upper), unused = lax.scan(
            cycle_step, (running, packed, packed), jnp.arange(1, reach_count + 1, dtype=jnp.int32)
        )
        return running

    initial_stats = (
        jnp.full((head_count, tok_dev), -1e30, jnp.float32),
        jnp.zeros((head_count, tok_dev), jnp.float32),
    )
    row_max, row_sum = sweep(add_stats, initial_stats)
    log_sum = row_max + jnp.log(row_sum)

    def add_output(out_acc, kv_block, k_place, k_docs):
        key_block = kv_block[:, :head_width]
        value_block = kv_block[:, head_width:]
        q_start, q_count = q_spans[0]
        live_mask = live_pairs(k_place, k_docs, q_start, q_count)

        def tile_output(q_start=q_start, q_count=q_count, live_mask=live_mask):
            scores = tile_scores(key_block)
            weights = jnp.where(
                live_mask[None],
                jnp.exp(scores - log_sum[:, q_start : q_start + q_count, None]),
                0.0,
            )
            probs = weights.astype(jnp.bfloat16)
            return jnp.einsum("hrk,kd->rhd", probs, value_block, preferred_element_type=jnp.float32)

        out_acc = out_acc.at[q_start : q_start + q_count].add(tile_output())
        return out_acc

    out_acc = sweep(add_output, jnp.zeros((tok_dev, head_count, head_width), jnp.float32))
    attention = out_acc.astype(jnp.bfloat16)
    delta = jnp.sum(cotangent.astype(jnp.float32) * attention.astype(jnp.float32), axis=2).T

    def grads_of(grad_q_acc, kv_block, k_place, k_docs):
        key_block = kv_block[:, :head_width]
        value_block = kv_block[:, head_width:]
        q_start, q_count = q_spans[0]
        live_mask = live_pairs(k_place, k_docs, q_start, q_count)

        def tile_grads(q_start=q_start, q_count=q_count, live_mask=live_mask):
            scores = tile_scores(key_block)
            weights = jnp.where(
                live_mask[None],
                jnp.exp(scores - log_sum[:, q_start : q_start + q_count, None]),
                0.0,
            )
            probs = weights.astype(jnp.bfloat16)
            dprobs = jnp.einsum(
                "rhd,kd->hrk", cotangent, value_block, preferred_element_type=jnp.float32
            )
            dscores = (
                weights * (dprobs - delta[:, q_start : q_start + q_count, None]) * score_scale
            ).astype(jnp.bfloat16)
            q_part = jnp.einsum(
                "hrk,kd->rhd", dscores, key_block, preferred_element_type=jnp.float32
            )
            k_part = jnp.einsum("hrk,rhd->kd", dscores, queries, preferred_element_type=jnp.float32)
            v_part = jnp.einsum("hrk,rhd->kd", probs, cotangent, preferred_element_type=jnp.float32)
            return (q_part, jnp.concatenate([k_part, v_part], axis=1))

        q_part, tile_part = tile_grads()
        grad_q_acc = grad_q_acc.at[q_start : q_start + q_count].add(q_part)
        return (grad_q_acc, tile_part)

    grad_q_acc, own_part = grads_of(
        jnp.zeros((tok_dev, head_count, head_width), jnp.float32), packed, q_place, q_docs
    )

    def back_step(carried, step_index):
        grad_q_acc, kv_lower, kv_upper = carried
        kv_lower = from_behind(kv_lower, "ctx", 1)
        kv_upper = from_behind(kv_upper, "ctx", -1)
        k_place, k_docs = positions((my_index - step_index) * tok_dev, tok_dev)
        grad_q_acc, lower_part = grads_of(grad_q_acc, kv_lower, k_place, k_docs)
        k_place, k_docs = positions((my_index + step_index) * tok_dev, tok_dev)
        grad_q_acc, upper_part = grads_of(grad_q_acc, kv_upper, k_place, k_docs)
        return ((grad_q_acc, kv_lower, kv_upper), (lower_part, upper_part))

    (grad_q_acc, kv_lower, kv_upper), (lower_parts, upper_parts) = lax.scan(
        back_step, (grad_q_acc, packed, packed), jnp.arange(1, reach_count + 1, dtype=jnp.int32)
    )
    from_lower = fold_home(lower_parts, False)
    from_upper = fold_home(upper_parts, True)
    kv_total = own_part + from_lower + from_upper
    kv_total = lax.psum(kv_total.astype(jnp.bfloat16), "head").astype(jnp.float32)
    kv_grads = kv_total.astype(jnp.bfloat16)
    attention_out = attention.reshape(tok_dev, head_count * head_width)
    grad_query = grad_q_acc.astype(jnp.bfloat16).reshape(tok_dev, head_count * head_width)
    return (attention_out, grad_query, kv_grads[:, :head_width], kv_grads[:, head_width:])


MESH = pl.DeviceIdType.MESH
NT = (((1,), (1,)), ((), ()))
TN = (((0,), (0,)), ((), ()))
NN = (((1,), (0,)), ((), ()))


def dot(lhs, rhs, dims):
    return lax.dot_general(lhs, rhs, dims, preferred_element_type=jnp.float32)


def near_kernel(
    n_ctx,
    n_head,
    lens_hbm,
    q_hbm,
    k_hbm,
    v_hbm,
    g_hbm,
    o_ref,
    dq_ref,
    dk_ref,
    dv_ref,
    lens_ref,
    q_ref,
    g_ref,
    kv_ref,
    halo_ref,
    own_part,
    own_send,
    halo_send,
    own_recv,
    halo_recv,
    final,
    load_sem,
    kv_send_sem,
    kv_recv_sem,
    own_send_sem,
    own_recv_sem,
    hs_send_sem,
    hs_recv_sem,
    fin_send_sem,
    fin_recv_sem,
):
    c = lax.axis_index("ctx")
    h = lax.axis_index("head")
    width = k_hbm.shape[1]
    tok = k_hbm.shape[0]
    st = tok // 2
    heads = q_hbm.shape[1] // width
    rows = heads * st
    quarter = tok // n_head
    per_half = n_head // 2
    has_prev = c > 0
    has_next = c < n_ctx - 1

    barrier = pltpu.get_barrier_semaphore()
    @pl.when(has_prev)
    def _():
        for d in range(n_head):
            pl.semaphore_signal(barrier, inc=1, device_id=(c - 1, d), device_id_type=MESH)

    @pl.when(has_next)
    def _():
        for d in range(n_head):
            pl.semaphore_signal(barrier, inc=1, device_id=(c + 1, d), device_id_type=MESH)

    for d in range(1, n_head):
        pl.semaphore_signal(
            barrier, inc=1, device_id=(c, lax.rem(h + d, n_head)), device_id_type=MESH
        )

    loads = [
        pltpu.make_async_copy(k_hbm, kv_ref.at[:, pl.ds(0, width)], load_sem.at[0]),
        pltpu.make_async_copy(v_hbm, kv_ref.at[:, pl.ds(width, width)], load_sem.at[1]),
        pltpu.make_async_copy(lens_hbm, lens_ref, load_sem.at[2]),
        pltpu.make_async_copy(q_hbm, q_ref, load_sem.at[3]),
        pltpu.make_async_copy(g_hbm, g_ref, load_sem.at[4]),
    ]
    for load in loads:
        load.start()

    loads[0].wait()
    loads[1].wait()
    pl.semaphore_wait(
        barrier,
        (n_head - 1) + n_head * has_prev.astype(jnp.int32) + n_head * has_next.astype(jnp.int32),
    )

    def kv_copy(part, step):
        return pltpu.make_async_remote_copy(
            src_ref=kv_ref.at[pl.ds(part * st, st), :],
            dst_ref=halo_ref.at[part],
            send_sem=kv_send_sem.at[part],
            recv_sem=kv_recv_sem.at[part],
            device_id=(c + step, h),
            device_id_type=MESH,
        )

    lower_kv, upper_kv = kv_copy(0, 1), kv_copy(1, -1)

    @pl.when(has_next)
    def _():
        lower_kv.start()

    @pl.when(has_prev)
    def _():
        upper_kv.start()

    loads[2].wait()
    lane = lax.broadcasted_iota(jnp.int32, (1, rows), 1)
    place = lax.rem(lane, st)
    key_row = lax.broadcasted_iota(jnp.int32, (2 * st, rows), 0)
    bases = (c * st, (2 * n_ctx - 1 - c) * st)
    starts = [jnp.zeros((1, rows), jnp.int32) for _ in bases]
    doc_end = jnp.int32(0)
    for doc in range(lens_ref.shape[0]):
        doc_end = doc_end + lens_ref[doc]
        for i, base in enumerate(bases):
            starts[i] = jnp.where(place + base >= doc_end, doc_end, starts[i])
    live = [
        (key_row + (base - st) >= start) & (key_row - st <= place)
        for base, start in zip(bases, starts)
    ]

    loads[3].wait()
    loads[4].wait()

    def stacked(ref, part):
        return jnp.concatenate(
            [
                ref[part * st : (part + 1) * st, i * width : (i + 1) * width]
                for i in range(heads)
            ],
            axis=0,
        )

    qs = [stacked(q_ref, part) for part in range(2)]
    gs = [stacked(g_ref, part) for part in range(2)]
    k_own = [kv_ref[part * st : (part + 1) * st, :width] for part in range(2)]
    v_own = [kv_ref[part * st : (part + 1) * st, width:] for part in range(2)]
    s_own = [dot(k_own[part], qs[part], NT) for part in range(2)]
    dp_own = [dot(v_own[part], gs[part], NT) for part in range(2)]

    @pl.when(has_prev)
    def _():
        lower_kv.wait_recv()

    @pl.when(has_next)
    def _():
        upper_kv.wait_recv()

    zero = jnp.zeros((st, 2 * width), jnp.bfloat16)
    halos = [
        jnp.where(has_prev, halo_ref[0], zero),
        jnp.where(has_next, halo_ref[1], kv_ref[0:st, :]),
    ]
    def halo_copy(part, j, step):
        return pltpu.make_async_remote_copy(
            src_ref=halo_send.at[part, pl.ds(j * quarter, quarter), :],
            dst_ref=halo_recv.at[h],
            send_sem=hs_send_sem.at[part, j],
            recv_sem=hs_recv_sem.at[h],
            device_id=(c + step, part * per_half + j),
            device_id_type=MESH,
        )

    down = [halo_copy(0, j, -1) for j in range(per_half)]
    up = [halo_copy(1, j, 1) for j in range(per_half)]
    scale = width ** (-0.5)
    probs, dscores, keys, values, grads = [], [], [], [], []
    for part in range(2):
        k_halo, v_halo = halos[part][:, :width], halos[part][:, width:]
        scores = jnp.concatenate([dot(k_halo, qs[part], NT), s_own[part]], axis=0) * scale
        dprobs = jnp.concatenate([dot(v_halo, gs[part], NT), dp_own[part]], axis=0)
        scores = jnp.where(live[part], scores, -1e30)
        peak = jnp.max(scores, axis=0, keepdims=True)
        raw = jnp.where(live[part], jnp.exp(scores - peak), 0.0)
        weights = raw * (1.0 / jnp.sum(raw, axis=0, keepdims=True))
        prob = weights.astype(jnp.bfloat16)
        delta = jnp.sum(prob.astype(jnp.float32) * dprobs, axis=0, keepdims=True)
        dscore = (weights * (dprobs - delta) * scale).astype(jnp.bfloat16)
        grad_k = dot(dscore, qs[part], NN)
        grad_v = dot(prob, gs[part], NN)
        probs.append(prob)
        dscores.append(dscore)
        keys.append(jnp.concatenate([k_halo, k_own[part]], axis=0))
        values.append(jnp.concatenate([v_halo, v_own[part]], axis=0))
        grads.append(jnp.concatenate([grad_k, grad_v], axis=1))
        halo_send[part] = grads[part][:st].astype(jnp.bfloat16)

        @pl.when((has_prev, has_next)[part])
        def _(part=part):
            for copy in (down, up)[part]:
                copy.start()


    lower = grads[0][st:] + jnp.where(has_next, 0.0, grads[1][:st])
    own_part[0:st, :] = lower
    own_part[st:tok, :] = grads[1][st:]
    own_send[0:st, :] = lower.astype(jnp.bfloat16)
    own_send[st:tok, :] = grads[1][st:].astype(jnp.bfloat16)
    own_copies = []
    for d in range(1, n_head):
        peer = lax.rem(h + d, n_head)
        own_copies.append(
            pltpu.make_async_remote_copy(
                src_ref=own_send.at[pl.ds(pl.multiple_of(peer * quarter, quarter), quarter), :],
                dst_ref=own_recv.at[d - 1],
                send_sem=own_send_sem.at[d - 1],
                recv_sem=own_recv_sem.at[d - 1],
                device_id=(c, peer),
                device_id_type=MESH,
            )
        )
    for copy in own_copies:
        copy.start()

    for part in range(2):
        out = dot(probs[part], values[part], TN).astype(jnp.bfloat16)
        grad_q = dot(dscores[part], keys[part], TN).astype(jnp.bfloat16)
        for i in range(heads):
            where = (slice(part * st, (part + 1) * st), slice(i * width, (i + 1) * width))
            o_ref[where] = out[i * st : (i + 1) * st]
            dq_ref[where] = grad_q[i * st : (i + 1) * st]

    mine = pl.ds(pl.multiple_of(h * quarter, quarter), quarter)
    gets_halo = jnp.where(h < per_half, has_next.astype(jnp.int32), has_prev.astype(jnp.int32))

    @pl.when(gets_halo == 1)
    def _():
        for j in range(n_head):
            pltpu.make_async_remote_copy(
                src_ref=halo_recv.at[j],
                dst_ref=halo_recv.at[j],
                send_sem=hs_send_sem.at[0, 0],
                recv_sem=hs_recv_sem.at[j],
                device_id=(c, lax.rem(h + 1, n_head)),
                device_id_type=MESH,
            ).wait_recv()

    total = own_part[mine, :]
    for d in range(n_head - 1):
        own_copies[d].wait_recv()
        total = total + own_recv[d].astype(jnp.float32)
    near = halo_recv[0].astype(jnp.float32)
    for j in range(1, n_head):
        near = near + halo_recv[j].astype(jnp.float32)
    total = total + jnp.where(gets_halo == 1, near, 0.0)
    final[mine, :] = total.astype(jnp.bfloat16)

    fin_copies = []
    for d in range(1, n_head):
        fin_copies.append(
            pltpu.make_async_remote_copy(
                src_ref=final.at[mine, :],
                dst_ref=final.at[mine, :],
                send_sem=fin_send_sem.at[d - 1],
                recv_sem=fin_recv_sem.at[d - 1],
                device_id=(c, lax.rem(h + d, n_head)),
                device_id_type=MESH,
            )
        )
    for copy in fin_copies:
        copy.start()

    @pl.when(has_next)
    def _():
        lower_kv.wait_send()
        for copy in up:
            copy.wait_send()

    @pl.when(has_prev)
    def _():
        upper_kv.wait_send()
        for copy in down:
            copy.wait_send()

    for copy in own_copies:
        copy.wait_send()
    for d in range(1, n_head):
        sender = lax.rem(h + n_head - d, n_head)
        theirs = pl.ds(pl.multiple_of(sender * quarter, quarter), quarter)
        pltpu.make_async_remote_copy(
            src_ref=final.at[theirs, :],
            dst_ref=final.at[theirs, :],
            send_sem=fin_send_sem.at[d - 1],
            recv_sem=fin_recv_sem.at[d - 1],
            device_id=(c, lax.rem(h + d, n_head)),
            device_id_type=MESH,
        ).wait_recv()
    dk_ref[...] = final[:, :width]
    dv_ref[...] = final[:, width:]
    for copy in fin_copies:
        copy.wait_send()


def write_kernel(*refs):
    sources, targets, sems = refs[:4], refs[4:8], refs[8]
    copies = [
        pltpu.make_async_copy(source, target, sems.at[i])
        for i, (source, target) in enumerate(zip(sources, targets))
    ]
    for copy in copies:
        copy.start()
    for copy in copies:
        copy.wait()


def near_body(n_ctx, n_head, query, key, value, grad_out, doc_lengths):
    tok, width = key.shape
    st = tok // 2
    quarter = tok // n_head
    bf16, f32 = jnp.bfloat16, jnp.float32
    dma = pltpu.SemaphoreType.DMA
    vmem = pl.BlockSpec(memory_space=pltpu.VMEM)
    hbm = pl.BlockSpec(memory_space=pltpu.HBM)
    results = pl.pallas_call(
        functools.partial(near_kernel, n_ctx, n_head),
        out_shape=(
            pltpu.VMEM(query.shape, bf16),
            pltpu.VMEM(query.shape, bf16),
            pltpu.VMEM(key.shape, bf16),
            pltpu.VMEM(key.shape, bf16),
        ),
        in_specs=[hbm] * 5,
        out_specs=(vmem,) * 4,
        scratch_shapes=[
            pltpu.SMEM(doc_lengths.shape, jnp.int32),
            pltpu.VMEM(query.shape, bf16),
            pltpu.VMEM(query.shape, bf16),
            pltpu.VMEM((tok, 2 * width), bf16),
            pltpu.VMEM((2, st, 2 * width), bf16),
            pltpu.VMEM((tok, 2 * width), f32),
            pltpu.VMEM((tok, 2 * width), bf16),
            pltpu.VMEM((2, st, 2 * width), bf16),
            pltpu.VMEM((n_head - 1, quarter, 2 * width), bf16),
            pltpu.VMEM((n_head, quarter, 2 * width), bf16),
            pltpu.VMEM((tok, 2 * width), bf16),
            dma((5,)),
            dma((2,)),
            dma((2,)),
            dma((n_head - 1,)),
            dma((n_head - 1,)),
            dma((2, n_head // 2)),
            dma((n_head,)),
            dma((n_head - 1,)),
            dma((n_head - 1,)),
        ],
        compiler_params=pltpu.CompilerParams(
            collective_id=0, has_side_effects=True, vmem_limit_bytes=60 * 1024 * 1024
        ),
    )(doc_lengths, query, key, value, grad_out)
    return pl.pallas_call(
        write_kernel,
        out_shape=tuple(jax.ShapeDtypeStruct(a.shape, bf16) for a in (query, query, key, key)),
        in_specs=[vmem] * 4,
        out_specs=(hbm,) * 4,
        scratch_shapes=[dma((4,))],
        compiler_params=pltpu.CompilerParams(vmem_limit_bytes=1024 * 1024),
        name="write_out",
    )(*results)


def solution(mesh):
    in_specs = (P("ctx", "head"), P("ctx", None), P("ctx", None), P("ctx", "head"), P())
    out_specs = (P("ctx", "head"), P("ctx", "head"), P("ctx", None), P("ctx", None))
    n_ctx, n_head = mesh.shape["ctx"], mesh.shape["head"]
    run = functools.partial(near_body, n_ctx, n_head) if n_ctx // 8 == 1 else body
    return jax.shard_map(run, mesh=mesh, in_specs=in_specs, out_specs=out_specs, check_vma=False)
```
